32 devices in a mesh: upd: 4 (over x, core), col: 8 (over z, y).
Axes of the slice: x: 2, y: 2, z: 4, core: 2. Of those that a mesh axis runs over, the one named last changes fastest.
Arguments:
- panel: bfloat16 [8, 8, 1024, 1024], P('col', None, 'upd'), may hold values from -6 to 6
- diag_tiles: bfloat16 [8, 1024, 1024], P('col', 'upd'), may hold values from -6 to 6
- dinv: bfloat16 [8, 1024, 1024], P('col'), may hold values from -1 to 1, as said below
- u_fac: bfloat16 [8, 8, 4, 96, 1024], P('col', None, 'upd'), may hold values from -1.1953125 to 1.1953125
- v_fac: bfloat16 [8, 8, 4, 96, 1024], P('col', None, 'upd'), may hold values from -1.1953125 to 1.1953125
- ranks: int32 [8, 8, 4], P('col', None, 'upd'), may hold values from 1 to 96, as said below
- sketch: bfloat16 [8, 64, 1024], P('col'), may hold values from -6 to 6
Outputs:
- panel_out: bfloat16 [8, 8, 1024, 1024], P('col', None, 'upd')
- diag_out: float32 [8, 1024, 1024], P('col', 'upd')
The draws below stay inside these ranges and needn't reach their ends.
Inputs may be any that keep to these rules, and one draw needn't show every extreme that they name: `ranks`: in every panel tile at least two of the 4 pieces have rank 96. `dinv`: each block is lower triangular with a positive diagonal.
All inputs are finite; a program needn't handle non-finite values.
Results may differ from the reference program's by a relative error of at most 0.014.
Values may be sent and summed in bfloat16 or wider, within the bound.
A program may use at most 64 MiB of HBM per device.

```python
import math
import jax
import jax.numpy as jnp
from jax import lax

B = 1024
RK = 64
MAXR = 96
BAND = 8
NCOL = 8
NUPD = 4


def draw_ranks(key, part):
    base = jax.random.fold_in(key, 11)
    key_a, key_b, key_c = jax.random.split(base, 3)
    shape = (NCOL, BAND, NUPD)
    scores = jax.random.randint(key_a, shape, 0, 1048576) * NUPD + jnp.arange(NUPD, dtype=jnp.int32)
    order = jnp.argsort(jnp.argsort(scores, axis=-1), axis=-1)
    first = jax.random.randint(key_b, shape, 0, MAXR)
    second = jax.random.randint(key_c, shape, 0, MAXR)
    rest = 1 + first * second // MAXR
    return jnp.where(order < 2, MAXR, rest).astype(jnp.int32)


def draw_dinv(key, part):
    base = jax.random.fold_in(key, 23)
    key_a, key_b = jax.random.split(base, 2)
    logd = jax.random.uniform(key_a, (NCOL, B), jnp.float32, math.log(0.5), math.log(2.0))
    diagonal = 0.075 * jnp.exp(logd)
    lower = jax.random.normal(key_b, (NCOL, B, B), jnp.float32) * (0.1 / math.sqrt(B))
    rows = jnp.arange(B, dtype=jnp.int32)[:, None]
    cols = jnp.arange(B, dtype=jnp.int32)[None, :]
    result = jnp.where(cols < rows, lower, 0.0) + jnp.where(cols == rows, diagonal[:, :, None], 0.0)
    return result.astype(jnp.bfloat16)


def shard_levels(own_key, shape, cuts, smallest, high):
    def one(axis_at, parts):
        steps = jax.random.uniform(jax.random.fold_in(jax.random.fold_in(own_key, 6), axis_at), (parts,), jnp.float32, smallest / len(cuts), high / len(cuts))
        return jnp.repeat(jnp.exp(steps), shape[axis_at] // parts).reshape((-1,) + (1,) * (len(shape) - axis_at - 1))

    loudness = one(*cuts[0])
    for cut in cuts[1:]:
        loudness = loudness * one(*cut)
    return loudness


def noise(stream_key, shape, scale, bound, shards=(), kind=jnp.bfloat16):
    drawn = scale * jax.random.normal(stream_key, shape, jnp.float32)
    if shards:
        drawn = drawn * shard_levels(stream_key, shape, shards, -0.22, 0.18)
    return jnp.clip(drawn, -bound, bound).astype(kind)


def setup_inputs(seed: int = 0) -> dict:
    streams_of = jax.random.split(jax.random.key(seed), 8)
    panel = noise(streams_of[0], (NCOL, BAND, B, B), 1.0, 6.0, ((0, 8), (2, 4)))
    diag_tiles = noise(streams_of[1], (NCOL, B, B), 1.0, 6.0, ((0, 8), (1, 4)))
    dinv = draw_dinv(jax.random.fold_in(streams_of[7], 71), 0)
    u_fac = noise(streams_of[3], (NCOL, BAND, NUPD, MAXR, B), 0.2, 1.1953125, ((0, 8), (2, 4)))
    v_fac = noise(streams_of[4], (NCOL, BAND, NUPD, MAXR, B), 0.2, 1.1953125, ((0, 8), (2, 4)))
    ranks = draw_ranks(jax.random.fold_in(streams_of[7], 71), 0)
    sketch = noise(streams_of[6], (NCOL, RK, B), 1.0, 6.0, ((0, 8),))
    return {"panel": panel, "diag_tiles": diag_tiles, "dinv": dinv, "u_fac": u_fac, "v_fac": v_fac, "ranks": ranks, "sketch": sketch}


def orthonormal(summed):
    gram = jnp.einsum('kb,lb->kl', summed, summed, precision=lax.Precision.HIGHEST)
    chol = jnp.linalg.cholesky(gram)
    return jax.scipy.linalg.solve_triangular(chol, summed, lower=True).astype(jnp.bfloat16)

def tile_factor(tile, left_factor, right_factor, piece_ranks, sketch_col, dinv_col):
    slots = jnp.arange(MAXR, dtype=jnp.int32)
    keep = slots[None, :, None] < piece_ranks[:, None, None]
    random_probe = jnp.einsum('urb,kb->urk', right_factor.astype(jnp.float32), sketch_col.astype(jnp.float32))
    random_probe = jnp.where(keep, random_probe, 0.0).astype(jnp.bfloat16)
    summed = jnp.einsum('urb,urk->kb', left_factor.astype(jnp.float32), random_probe.astype(jnp.float32))
    range_basis = orthonormal(summed)
    coefficient_matrix = jnp.einsum('urb,kb->urk', left_factor.astype(jnp.float32), range_basis.astype(jnp.float32))
    coefficient_matrix = jnp.where(keep, coefficient_matrix, 0.0).astype(jnp.bfloat16)
    cross_term = jnp.einsum('urb,urk->kb', right_factor.astype(jnp.float32), coefficient_matrix.astype(jnp.float32)).astype(jnp.bfloat16)
    approximation = jnp.dot(range_basis.T.astype(jnp.float32), cross_term.astype(jnp.float32), preferred_element_type=jnp.float32)
    updated_tile = (tile.astype(jnp.float32) - approximation).astype(jnp.bfloat16)
    return jnp.dot(updated_tile.astype(jnp.float32), dinv_col.T.astype(jnp.float32), preferred_element_type=jnp.float32).astype(jnp.bfloat16)

def column_factor(pack):
    tiles, dinv_col, left_factor, right_factor, col_ranks, sketch_col = pack
    solve = lambda tile, lf, rf, rk: tile_factor(tile, lf, rf, rk, sketch_col, dinv_col)
    return jax.vmap(solve)(tiles, left_factor, right_factor, col_ranks)

def reference(panel, diag_tiles, dinv, u_fac, v_fac, ranks, sketch):
    factors = lax.map(column_factor, (panel, dinv, u_fac, v_fac, ranks, sketch))
    accum = diag_tiles.astype(jnp.float32)
    for shift_by in range(1, BAND + 1):
        if shift_by < NCOL:
            moved = factors[:NCOL - shift_by, shift_by - 1].astype(jnp.float32)
            accum = accum.at[shift_by:].add(-jnp.einsum('jrb,jnb->jrn', moved, moved))
    return (factors, accum)
```

```python
import functools

import jax
import jax.numpy as jnp
from jax import lax
from jax.experimental import pallas as pl
from jax.experimental.pallas import tpu as pltpu
from jax.sharding import PartitionSpec as P

F32 = jnp.float32
BF16 = jnp.bfloat16
NT = (((1,), (1,)), ((), ()))
TN = (((0,), (0,)), ((), ()))
NN = (((1,), (0,)), ((), ()))


def dot(a, b, dims):
    return lax.dot_general(a, b, dims, preferred_element_type=F32)


def dot_high(a, b, dims):
    return lax.dot_general(
        a, b, dims, precision=lax.Precision.HIGHEST, preferred_element_type=F32
    )


def inverse_factor(aug):
    size = aug.shape[1]
    rows = lax.broadcasted_iota(jnp.int32, (1, size, 1), 1)
    for j in range(size - 1):
        pivot = aug[:, j : j + 1, :]
        scaled = pivot / aug[:, j : j + 1, j : j + 1]
        column = jnp.where(rows > j, aug[:, :, j : j + 1], 0.0)
        aug = aug - column * scaled
    at_row = lax.broadcasted_iota(jnp.int32, (1, size, 2 * size), 1)
    at_col = lax.broadcasted_iota(jnp.int32, (1, size, 2 * size), 2)
    diagonal = jnp.sum(jnp.where(at_row == at_col, aug, 0.0), axis=2, keepdims=True)
    return jnp.where(at_col >= size, aug / jnp.sqrt(diagonal), 0.0)


def kernel(
    U, C,
    panel, diag, dinv, uf, vf, keep, sketch,
    out, diag_out,
    t0f, t0b, rx, bx, ex, r, r_rx, basis, xp, x_rx, e, tc, part, p_rx,
    t_s, t_r, bx_s, bx_r, ex_s, ex_r, r_s, r_r, b_s, b_r, x_s, x_r, e_s, e_r, p_s, p_r,
):
    M, RD, B = panel.shape[1:]
    K = sketch.shape[1]
    CB = B // U
    MT = M // U
    me_u, me_c = lax.axis_index("upd"), lax.axis_index("col")

    def copy(src, dst, send, recv, u, c):
        return pltpu.make_async_remote_copy(
            src_ref=src, dst_ref=dst, send_sem=send, recv_sem=recv,
            device_id={"upd": u, "col": c}, device_id_type=pl.DeviceIdType.MESH,
        )

    def after(k):
        return lax.rem(me_u + k, U)

    def before(k):
        return lax.rem(me_u + U - k, U)

    own = pl.ds(me_u * MT, MT)

    def tiles(u):
        return pl.ds(u * MT, MT)

    def to_column(m):
        return me_c + m + 1

    barrier = pltpu.get_barrier_semaphore()

    def greet(u, c):
        pl.semaphore_signal(
            barrier, inc=1, device_id={"upd": u, "col": c}, device_id_type=pl.DeviceIdType.MESH
        )

    for k in range(1, U):
        greet(after(k), me_c)

    @pl.loop(0, M)
    def _(m):
        @pl.when(me_c + m + 1 < C)
        def _():
            for v in range(U):
                greet(v, me_c + m + 1)

        @pl.when(me_c - m - 1 >= 0)
        def _():
            for v in range(U):
                greet(v, me_c - m - 1)

    @pl.loop(0, M)
    def _(t):
        probe = (dot(sketch[0], vf[0, t, 0], NT) * keep[t]).astype(BF16)
        r[t] = dot(probe, uf[0, t, 0], NN).astype(BF16)

    pl.semaphore_wait(
        barrier, U - 1 + U * (jnp.minimum(M, C - 1 - me_c) + jnp.minimum(M, me_c))
    )

    def scatter_out(buf, k, land, send, recv):
        return copy(
            buf.at[tiles(after(k))], land.at[k - 1], send.at[k - 1], recv.at[k - 1], after(k), me_c
        )

    for k in range(1, U):
        scatter_out(r, k, r_rx, r_s, r_r).start()

    def t_copy(m, v):
        return copy(
            t0b.at[m, v], rx.at[m, pl.ds(me_u * RD, RD)],
            t_s.at[m, v], t_r.at[m, me_u], v, to_column(m),
        )

    @pl.loop(0, M)
    def _(m):
        for v in range(U):
            block = dot(panel[0, m], dinv[0, v * CB : (v + 1) * CB, :], NT)
            t0f[m, :, v * CB : (v + 1) * CB] = block
            t0b[m, v] = block.astype(BF16)

        @pl.when(to_column(m) < C)
        def _():
            for v in range(U):
                t_copy(m, v).start()

    for k in range(1, U):
        scatter_out(r, k, r_rx, r_s, r_r).wait_recv()

    summed = r[own].astype(F32)
    for k in range(1, U):
        summed = summed + r_rx[k - 1].astype(F32)
    zeros = jnp.zeros((K, B), F32)
    at_row = lax.broadcasted_iota(jnp.int32, (K, 2 * K), 0)
    at_col = lax.broadcasted_iota(jnp.int32, (K, 2 * K), 1)
    eye = jnp.where(at_col == at_row + K, 1.0, 0.0).astype(F32)
    grams = [
        dot_high(summed[i], jnp.concatenate([summed[i], zeros], axis=0), NT) + eye
        for i in range(MT)
    ]
    inverse = inverse_factor(jnp.stack(grams))
    for i in range(MT):
        basis[me_u * MT + i] = dot_high(
            inverse[i], jnp.concatenate([zeros, summed[i]], axis=0), NN
        ).astype(BF16)

    def gather_out(buf, k, send, recv):
        return copy(buf.at[own], buf.at[own], send.at[k - 1], recv.at[k - 1], after(k), me_c)

    def gather_in(buf, k, send, recv):
        region = buf.at[tiles(before(k))]
        return copy(region, region, send.at[k - 1], recv.at[k - 1], after(k), me_c)

    for k in range(1, U):
        gather_out(basis, k, b_s, b_r).start()
    for k in range(1, U):
        gather_in(basis, k, b_s, b_r).wait_recv()

    def project(t):
        coeff = (dot(basis[t], uf[0, t, 0], NT) * keep[t]).astype(BF16)
        xp[t] = dot(coeff, vf[0, t, 0], NN).astype(BF16)

    @pl.loop(0, M)
    def _(t):
        project(t)

    for k in range(1, U):
        scatter_out(xp, k, x_rx, x_s, x_r).start()

    def b_copy(m):
        return copy(basis.at[m], bx.at[m], bx_s.at[m], bx_r.at[m], me_u, to_column(m))

    @pl.loop(0, M)
    def _(m):
        @pl.when(to_column(m) < C)
        def _():
            b_copy(m).start()

    for k in range(1, U):
        scatter_out(xp, k, x_rx, x_s, x_r).wait_recv()

    cross = xp[own].astype(F32)
    for k in range(1, U):
        cross = cross + x_rx[k - 1].astype(F32)
    cross = cross.astype(BF16)
    for i in range(MT):
        for v in range(U):
            e[me_u * MT + i, v] = dot(
                cross[i], dinv[0, v * CB : (v + 1) * CB, :], NT
            ).astype(BF16)

    def e_copy(i, v):
        m = me_u * MT + i
        return copy(e.at[m, v], ex.at[m], ex_s.at[i, v], ex_r.at[m], v, to_column(m))

    for i in range(MT):
        @pl.when(to_column(me_u * MT + i) < C)
        def _():
            for v in range(U):
                e_copy(i, v).start()

    for k in range(1, U):
        gather_out(e, k, e_s, e_r).start()
    for k in range(1, U):
        gather_in(e, k, e_s, e_r).wait_recv()

    @pl.loop(0, M)
    def _(m):
        rows = basis[m, :, pl.ds(pl.multiple_of(me_u * RD, RD), RD)]
        for v in range(U):
            cols = slice(v * CB, (v + 1) * CB)
            out[0, m, :, cols] = (t0f[m, :, cols] - dot(rows, e[m, v], TN)).astype(BF16)

    for m in range(M):
        cols = slice(m * CB, (m + 1) * CB)

        @pl.when(me_c - m - 1 >= 0)
        def _():
            @pl.loop(0, U)
            def _(s):
                copy(
                    t0b.at[m, 0], rx.at[m, pl.ds(s * RD, RD)],
                    t_s.at[m, 0], t_r.at[m, s], me_u, me_c,
                ).wait_recv()

            b_copy(m).wait_recv()
            copy(e.at[m, 0], ex.at[m], ex_s.at[0, 0], ex_r.at[m], me_u, me_c).wait_recv()

            @pl.loop(0, U)
            def _(s):
                rows = pl.ds(pl.multiple_of(s * RD, RD), RD)
                change = dot(bx[m, :, rows], ex[m], TN)
                tc[rows, cols] = (rx[m, rows, :].astype(F32) - change).astype(BF16)

        @pl.when(me_c - m - 1 < 0)
        def _():
            tc[:, cols] = jnp.zeros((B, CB), BF16)

    def p_copy(k):
        return copy(
            part.at[k - 1], p_rx.at[k - 1], p_s.at[k - 1], p_r.at[k - 1], after(k), me_c
        )

    def product(u):
        return dot(tc[pl.ds(pl.multiple_of(u * RD, RD), RD), :], tc[...], NT)

    @pl.loop(1, U)
    def _(k):
        part[k - 1] = product(after(k)).astype(BF16)
        p_copy(k).start()

    diag_out[0] = diag[0].astype(F32) - product(me_u)
    for k in range(1, U):
        p_copy(k).wait_recv()
        diag_out[0] = diag_out[0] - p_rx[k - 1].astype(F32)

    for k in range(1, U):
        scatter_out(r, k, r_rx, r_s, r_r).wait_send()
        gather_out(basis, k, b_s, b_r).wait_send()
        scatter_out(xp, k, x_rx, x_s, x_r).wait_send()
        gather_out(e, k, e_s, e_r).wait_send()
        p_copy(k).wait_send()
    for i in range(MT):
        @pl.when(to_column(me_u * MT + i) < C)
        def _():
            for v in range(U):
                e_copy(i, v).wait_send()

    @pl.loop(0, M)
    def _(m):
        @pl.when(to_column(m) < C)
        def _():
            for v in range(U):
                t_copy(m, v).wait_send()
            b_copy(m).wait_send()


def local(U, C, panel, diag_tiles, dinv, u_fac, v_fac, ranks, sketch):
    M, RD, B = panel.shape[1:]
    R = u_fac.shape[3]
    K = sketch.shape[1]
    CB, MT = B // U, M // U
    slots = lax.broadcasted_iota(jnp.int32, (M, 1, R), 2)
    keep = (slots < ranks[0, :, 0][:, None, None]).astype(F32)
    dma = pltpu.SemaphoreType.DMA
    peers = [dma((U - 1,))] * 2
    vmem = pl.BlockSpec(memory_space=pltpu.VMEM)
    return pl.pallas_call(
        functools.partial(kernel, U, C),
        out_shape=(
            jax.ShapeDtypeStruct(panel.shape, BF16),
            jax.ShapeDtypeStruct(diag_tiles.shape, F32),
        ),
        in_specs=[vmem] * 7,
        out_specs=(vmem, vmem),
        scratch_shapes=[
            pltpu.VMEM((M, RD, B), F32),
            pltpu.VMEM((M, U, RD, CB), BF16),
            pltpu.VMEM((M, B, CB), BF16),
            pltpu.VMEM((M, K, B), BF16),
            pltpu.VMEM((M, K, CB), BF16),
            pltpu.VMEM((M, K, B), BF16),
            pltpu.VMEM((U - 1, MT, K, B), BF16),
            pltpu.VMEM((M, K, B), BF16),
            pltpu.VMEM((M, K, B), BF16),
            pltpu.VMEM((U - 1, MT, K, B), BF16),
            pltpu.VMEM((M, U, K, CB), BF16),
            pltpu.VMEM((B, M * CB), BF16),
            pltpu.VMEM((U - 1, RD, B), BF16),
            pltpu.VMEM((U - 1, RD, B), BF16),
            dma((M, U)), dma((M, U)), dma((M,)), dma((M,)), dma((MT, U)), dma((M,)),
            *peers, *peers, *peers, *peers, *peers,
        ],
        compiler_params=pltpu.CompilerParams(
            collective_id=0, has_side_effects=True, vmem_limit_bytes=58 * 1024 * 1024
        ),
        name="band_window",
    )(panel, diag_tiles, dinv, u_fac, v_fac, keep, sketch)


def solution(mesh):
    in_specs = (
        P("col", None, "upd", None),
        P("col", "upd", None),
        P("col", None, None),
        P("col", None, "upd", None, None),
        P("col", None, "upd", None, None),
        P("col", None, "upd"),
        P("col", None, None),
    )
    out_specs = (P("col", None, "upd", None), P("col", "upd", None))
    body = functools.partial(local, mesh.shape["upd"], mesh.shape["col"])
    return jax.shard_map(body, mesh=mesh, in_specs=in_specs, out_specs=out_specs, check_vma=False)
```

```python
import functools

import jax
import jax.numpy as jnp
from jax import lax
from jax.experimental import pallas as pl
from jax.experimental.pallas import tpu as pltpu
from jax.sharding import PartitionSpec as P

F32 = jnp.float32
BF16 = jnp.bfloat16
NT = (((1,), (1,)), ((), ()))
TN = (((0,), (0,)), ((), ()))
NN = (((1,), (0,)), ((), ()))


def dot(a, b, dims):
    return lax.dot_general(a, b, dims, preferred_element_type=F32)


def dot_high(a, b, dims):
    return lax.dot_general(
        a, b, dims, precision=lax.Precision.HIGHEST, preferred_element_type=F32
    )


def inverse_factor(aug):
    size = aug.shape[1]
    rows = lax.broadcasted_iota(jnp.int32, (1, size, 1), 1)
    for j in range(size - 1):
        pivot = aug[:, j : j + 1, :]
        scaled = pivot / aug[:, j : j + 1, j : j + 1]
        column = jnp.where(rows > j, aug[:, :, j : j + 1], 0.0)
        aug = aug - column * scaled
    at_row = lax.broadcasted_iota(jnp.int32, (1, size, 2 * size), 1)
    at_col = lax.broadcasted_iota(jnp.int32, (1, size, 2 * size), 2)
    diagonal = jnp.sum(jnp.where(at_row == at_col, aug, 0.0), axis=2, keepdims=True)
    return jnp.where(at_col >= size, aug / jnp.sqrt(diagonal), 0.0)


def kernel(
    U, C,
    panel, diag, dinv, uf, vf, keep, sketch,
    out, diag_out,
    t0f, t0b, tc, bf, f, r, r_rx, basis, xp, x_rx, e, acc, near, near_rx, far, far_rx,
    t_s, t_r, bx_s, bx_r, f_s, f_r, r_s, r_r, b_s, b_r, x_s, x_r, e_s, e_r,
    near_s, near_r, far_s, far_r,
):
    M, RD, B = panel.shape[1:]
    K = sketch.shape[1]
    CB = B // U
    MT = M // U
    me_u, me_c = lax.axis_index("upd"), lax.axis_index("col")

    def copy(src, dst, send, recv, u, c):
        return pltpu.make_async_remote_copy(
            src_ref=src, dst_ref=dst, send_sem=send, recv_sem=recv,
            device_id={"upd": u, "col": c}, device_id_type=pl.DeviceIdType.MESH,
        )

    def after(k):
        return lax.rem(me_u + k, U)

    def before(k):
        return lax.rem(me_u + U - k, U)

    own = pl.ds(me_u * MT, MT)

    def tiles(u):
        return pl.ds(u * MT, MT)

    def to_column(m):
        return me_c + m + 1

    barrier = pltpu.get_barrier_semaphore()

    def greet(u, c):
        pl.semaphore_signal(
            barrier, inc=1, device_id={"upd": u, "col": c}, device_id_type=pl.DeviceIdType.MESH
        )

    for k in range(1, U):
        greet(after(k), me_c)

    @pl.loop(0, M)
    def _(m):
        @pl.when(me_c + m + 1 < C)
        def _():
            for v in range(U):
                greet(v, me_c + m + 1)

        @pl.when(me_c - m - 1 >= 0)
        def _():
            for v in range(U):
                greet(v, me_c - m - 1)

    @pl.loop(0, M)
    def _(t):
        probe = (dot(sketch[0], vf[0, t, 0], NT) * keep[t]).astype(BF16)
        r[t] = dot(probe, uf[0, t, 0], NN).astype(BF16)

    pl.semaphore_wait(
        barrier, U - 1 + U * (jnp.minimum(M, C - 1 - me_c) + jnp.minimum(M, me_c))
    )

    def scatter_out(buf, k, land, send, recv):
        return copy(
            buf.at[tiles(after(k))], land.at[k - 1], send.at[k - 1], recv.at[k - 1], after(k), me_c
        )

    for k in range(1, U):
        scatter_out(r, k, r_rx, r_s, r_r).start()

    def t_copy(m, v):
        return copy(
            t0b.at[m, v],
            tc.at[pl.ds(me_u * RD, RD), pl.ds(pl.multiple_of(m * CB, CB), CB)],
            t_s.at[m, v], t_r.at[m, me_u], v, to_column(m),
        )

    @pl.loop(0, M)
    def _(m):
        for v in range(U):
            block = dot(panel[0, m], dinv[0, v * CB : (v + 1) * CB, :], NT)
            t0f[m, :, v * CB : (v + 1) * CB] = block
            t0b[m, v] = block.astype(BF16)

        @pl.when(to_column(m) < C)
        def _():
            for v in range(U):
                t_copy(m, v).start()

    for k in range(1, U):
        scatter_out(r, k, r_rx, r_s, r_r).wait_recv()

    summed = r[own].astype(F32)
    for k in range(1, U):
        summed = summed + r_rx[k - 1].astype(F32)
    zeros = jnp.zeros((K, B), F32)
    at_row = lax.broadcasted_iota(jnp.int32, (K, 2 * K), 0)
    at_col = lax.broadcasted_iota(jnp.int32, (K, 2 * K), 1)
    eye = jnp.where(at_col == at_row + K, 1.0, 0.0).astype(F32)
    grams = [
        dot_high(summed[i], jnp.concatenate([summed[i], zeros], axis=0), NT) + eye
        for i in range(MT)
    ]
    inverse = inverse_factor(jnp.stack(grams))
    for i in range(MT):
        basis[me_u * MT + i] = dot_high(
            inverse[i], jnp.concatenate([zeros, summed[i]], axis=0), NN
        ).astype(BF16)

    def gather_out(buf, k, send, recv):
        return copy(buf.at[own], buf.at[own], send.at[k - 1], recv.at[k - 1], after(k), me_c)

    def gather_in(buf, k, send, recv):
        region = buf.at[tiles(before(k))]
        return copy(region, region, send.at[k - 1], recv.at[k - 1], after(k), me_c)

    for k in range(1, U):
        gather_out(basis, k, b_s, b_r).start()

    def b_copy(i):
        m = me_u * MT + i
        return copy(basis.at[m], bf.at[i, 0], bx_s.at[i], bx_r.at[i], me_u, to_column(m))

    for i in range(MT):
        @pl.when(to_column(me_u * MT + i) < C)
        def _():
            b_copy(i).start()

    for k in range(1, U):
        gather_in(basis, k, b_s, b_r).wait_recv()

    def project(t):
        coeff = (dot(basis[t], uf[0, t, 0], NT) * keep[t]).astype(BF16)
        xp[t] = dot(coeff, vf[0, t, 0], NN).astype(BF16)

    @pl.loop(0, M)
    def _(t):
        project(t)

    for k in range(1, U):
        scatter_out(xp, k, x_rx, x_s, x_r).start()

    for k in range(1, U):
        scatter_out(xp, k, x_rx, x_s, x_r).wait_recv()

    cross = xp[own].astype(F32)
    for k in range(1, U):
        cross = cross + x_rx[k - 1].astype(F32)
    cross = cross.astype(BF16)
    for i in range(MT):
        for v in range(U):
            e[me_u * MT + i, v] = dot(
                cross[i], dinv[0, v * CB : (v + 1) * CB, :], NT
            ).astype(BF16)

    for k in range(1, U):
        gather_out(e, k, e_s, e_r).start()
    for k in range(1, U):
        gather_in(e, k, e_s, e_r).wait_recv()

    def f_copy(m, i):
        return copy(
            f.at[m], bf.at[i, 1, :, pl.ds(pl.multiple_of(me_u * RD, RD), RD)],
            f_s.at[m], f_r.at[i, me_u], m // MT, to_column(m),
        )

    for m in range(M):
        @pl.when(to_column(m) < C)
        def _():
            rows = basis[m, :, pl.ds(pl.multiple_of(me_u * RD, RD), RD)]
            left = jnp.zeros((K, RD), F32)
            square = jnp.zeros((K, K), F32)
            for v in range(U):
                left = left + dot(e[m, v], t0b[m, v], NT)
                square = square + dot(e[m, v], e[m, v], NT)
            f[m] = (left - 0.5 * dot_high(square, rows.astype(F32), NN)).astype(BF16)
            f_copy(m, m % MT).start()

    @pl.loop(0, M)
    def _(m):
        rows = basis[m, :, pl.ds(pl.multiple_of(me_u * RD, RD), RD)]
        for v in range(U):
            cols = slice(v * CB, (v + 1) * CB)
            out[0, m, :, cols] = (t0f[m, :, cols] - dot(rows, e[m, v], TN)).astype(BF16)

    for m in range(M):
        cols = slice(m * CB, (m + 1) * CB)

        @pl.when(me_c - m - 1 >= 0)
        def _():
            @pl.loop(0, U)
            def _(s):
                copy(
                    t0b.at[m, 0], tc.at[pl.ds(s * RD, RD), cols],
                    t_s.at[m, 0], t_r.at[m, s], me_u, me_c,
                ).wait_recv()

        @pl.when(me_c - m - 1 < 0)
        def _():
            tc[:, cols] = jnp.zeros((B, CB), BF16)

    def rows_of(u):
        return pl.ds(pl.multiple_of(u * RD, RD), RD)

    @pl.loop(0, U)
    def _(u):
        acc[rows_of(u), :] = dot(tc[rows_of(u), :], tc[...], NT)

    for i in range(MT):
        @pl.when(me_c - (me_u * MT + i) - 1 >= 0)
        def _():
            b_copy(i).wait_recv()

            @pl.loop(0, U)
            def _(s):
                copy(
                    f.at[0], bf.at[i, 1, :, pl.ds(pl.multiple_of(s * RD, RD), RD)],
                    f_s.at[0], f_r.at[i, s], me_u, me_c,
                ).wait_recv()

        @pl.when(me_c - (me_u * MT + i) - 1 < 0)
        def _():
            bf[i] = jnp.zeros((2, K, B), BF16)

    def product(u):
        total = acc[rows_of(u), :]
        for i in range(MT):
            total = total - dot(bf[i, 0, :, rows_of(u)], bf[i, 1], TN)
            total = total - dot(bf[i, 1, :, rows_of(u)], bf[i, 0], TN)
        return total

    X = U // 2
    side = lax.rem(me_u, 2)
    partner = me_u + 1 - 2 * side

    def ahead(k):
        return lax.rem(me_u + 2 * k, U)

    def near_copy(k):
        return copy(near.at[k], near_rx.at[k], near_s.at[k], near_r.at[k], partner, me_c)

    def far_copy(k):
        return copy(
            far.at[k - 1], far_rx.at[k - 1], far_s.at[k - 1], far_r.at[k - 1], ahead(k), me_c
        )

    for n in range(1, X + 1):
        k = n % X
        near[k] = product(ahead(k) + 1 - 2 * side).astype(BF16)
        near_copy(k).start()
    for k in range(1, X):
        part = product(ahead(k))
        near_copy(k).wait_recv()
        far[k - 1] = (part + near_rx[k].astype(F32)).astype(BF16)
        far_copy(k).start()
    part = diag[0].astype(F32) - product(me_u)
    near_copy(0).wait_recv()
    diag_out[0] = part - near_rx[0].astype(F32)
    for k in range(1, X):
        far_copy(k).wait_recv()
        diag_out[0] = diag_out[0] - far_rx[k - 1].astype(F32)

    for k in range(1, U):
        scatter_out(r, k, r_rx, r_s, r_r).wait_send()
        gather_out(basis, k, b_s, b_r).wait_send()
        scatter_out(xp, k, x_rx, x_s, x_r).wait_send()
        gather_out(e, k, e_s, e_r).wait_send()
    for k in range(X):
        near_copy(k).wait_send()
    for k in range(1, X):
        far_copy(k).wait_send()
    for i in range(MT):
        @pl.when(to_column(me_u * MT + i) < C)
        def _():
            b_copy(i).wait_send()

    @pl.loop(0, M)
    def _(m):
        @pl.when(to_column(m) < C)
        def _():
            for v in range(U):
                t_copy(m, v).wait_send()
            f_copy(m, lax.rem(m, MT)).wait_send()


def local(U, C, panel, diag_tiles, dinv, u_fac, v_fac, ranks, sketch):
    M, RD, B = panel.shape[1:]
    R = u_fac.shape[3]
    K = sketch.shape[1]
    CB, MT, X = B // U, M // U, U // 2
    slots = lax.broadcasted_iota(jnp.int32, (M, 1, R), 2)
    keep = (slots < ranks[0, :, 0][:, None, None]).astype(F32)
    dma = pltpu.SemaphoreType.DMA
    peers = [dma((U - 1,))] * 2
    vmem = pl.BlockSpec(memory_space=pltpu.VMEM)
    return pl.pallas_call(
        functools.partial(kernel, U, C),
        out_shape=(
            jax.ShapeDtypeStruct(panel.shape, BF16),
            jax.ShapeDtypeStruct(diag_tiles.shape, F32),
        ),
        in_specs=[vmem] * 7,
        out_specs=(vmem, vmem),
        scratch_shapes=[
            pltpu.VMEM((M, RD, B), F32),
            pltpu.VMEM((M, U, RD, CB), BF16),
            pltpu.VMEM((B, M * CB), BF16),
            pltpu.VMEM((MT, 2, K, B), BF16),
            pltpu.VMEM((M, K, RD), BF16),
            pltpu.VMEM((M, K, B), BF16),
            pltpu.VMEM((U - 1, MT, K, B), BF16),
            pltpu.VMEM((M, K, B), BF16),
            pltpu.VMEM((M, K, B), BF16),
            pltpu.VMEM((U - 1, MT, K, B), BF16),
            pltpu.VMEM((M, U, K, CB), BF16),
            pltpu.VMEM((B, B), F32),
            pltpu.VMEM((X, RD, B), BF16),
            pltpu.VMEM((X, RD, B), BF16),
            pltpu.VMEM((X - 1, RD, B), BF16),
            pltpu.VMEM((X - 1, RD, B), BF16),
            dma((M, U)), dma((M, U)), dma((MT,)), dma((MT,)), dma((M,)), dma((MT, U)),
            *peers, *peers, *peers, *peers,
            dma((X,)), dma((X,)), dma((X - 1,)), dma((X - 1,)),
        ],
        compiler_params=pltpu.CompilerParams(
            collective_id=0, has_side_effects=True, vmem_limit_bytes=58 * 1024 * 1024
        ),
        name="band_window",
    )(panel, diag_tiles, dinv, u_fac, v_fac, keep, sketch)


def solution(mesh):
    in_specs = (
        P("col", None, "upd", None),
        P("col", "upd", None),
        P("col", None, None),
        P("col", None, "upd", None, None),
        P("col", None, "upd", None, None),
        P("col", None, "upd"),
        P("col", None, None),
    )
    out_specs = (P("col", None, "upd", None), P("col", "upd", None))
    body = functools.partial(local, mesh.shape["upd"], mesh.shape["col"])
    return jax.shard_map(body, mesh=mesh, in_specs=in_specs, out_specs=out_specs, check_vma=False)
```

```python
import functools

import jax
import jax.numpy as jnp
from jax import lax
from jax.experimental import pallas as pl
from jax.experimental.pallas import tpu as pltpu
from jax.sharding import PartitionSpec as P

F32 = jnp.float32
BF16 = jnp.bfloat16
NT = (((1,), (1,)), ((), ()))
TN = (((0,), (0,)), ((), ()))
NN = (((1,), (0,)), ((), ()))


def dot(a, b, dims):
    return lax.dot_general(a, b, dims, preferred_element_type=F32)


def dot_high(a, b, dims):
    return lax.dot_general(
        a, b, dims, precision=lax.Precision.HIGHEST, preferred_element_type=F32
    )


def inverse_factor(aug):
    size = aug.shape[1]
    rows = lax.broadcasted_iota(jnp.int32, (1, size, 1), 1)
    for j in range(size - 1):
        pivot = aug[:, j : j + 1, :]
        scaled = pivot / aug[:, j : j + 1, j : j + 1]
        column = jnp.where(rows > j, aug[:, :, j : j + 1], 0.0)
        aug = aug - column * scaled
    at_row = lax.broadcasted_iota(jnp.int32, (1, size, 2 * size), 1)
    at_col = lax.broadcasted_iota(jnp.int32, (1, size, 2 * size), 2)
    diagonal = jnp.sum(jnp.where(at_row == at_col, aug, 0.0), axis=2, keepdims=True)
    return jnp.where(at_col >= size, aug / jnp.sqrt(diagonal), 0.0)


def kernel(
    U, C,
    panel, diag, dinv, uf, vf, keep, sketch,
    out, diag_out,
    t0f, t0b, tx, tc, bf, pair, f, r, r_rx, basis, xp, x_rx, e, acc, near, near_rx, far, far_rx,
    g_s, g_r, t_s, t_r, bx_s, bx_r, f_s, f_r, r_s, r_r, b_s, b_r, x_s, x_r, e_s, e_r,
    near_s, near_r, far_s, far_r,
):
    M, RD, B = panel.shape[1:]
    K = sketch.shape[1]
    CB = B // U
    MT = M // U
    me_u, me_c = lax.axis_index("upd"), lax.axis_index("col")

    def copy(src, dst, send, recv, u, c):
        return pltpu.make_async_remote_copy(
            src_ref=src, dst_ref=dst, send_sem=send, recv_sem=recv,
            device_id={"upd": u, "col": c}, device_id_type=pl.DeviceIdType.MESH,
        )

    def after(k):
        return lax.rem(me_u + k, U)

    def before(k):
        return lax.rem(me_u + U - k, U)

    own = pl.ds(me_u * MT, MT)

    def tiles(u):
        return pl.ds(u * MT, MT)

    def to_column(m):
        return me_c + m + 1

    barrier = pltpu.get_barrier_semaphore()

    def greet(u, c):
        pl.semaphore_signal(
            barrier, inc=1, device_id={"upd": u, "col": c}, device_id_type=pl.DeviceIdType.MESH
        )

    for k in range(1, U):
        greet(after(k), me_c)

    @pl.loop(0, M)
    def _(m):
        @pl.when(me_c + m + 1 < C)
        def _():
            for v in range(U):
                greet(v, me_c + m + 1)

        @pl.when(me_c - m - 1 >= 0)
        def _():
            for v in range(U):
                greet(v, me_c - m - 1)

    pl.semaphore_wait(
        barrier, U - 1 + U * (jnp.minimum(M, C - 1 - me_c) + jnp.minimum(M, me_c))
    )

    def scatter_out(buf, k, land, send, recv):
        return copy(
            buf.at[tiles(after(k))], land.at[k - 1], send.at[k - 1], recv.at[k - 1], after(k), me_c
        )

    def rows_of(u):
        return pl.ds(pl.multiple_of(u * RD, RD), RD)

    sends = jnp.minimum(M, C - 1 - me_c)

    def tile(n):
        return lax.rem(sends - 1 - n + M, M)

    def g_copy(m, k):
        return copy(
            t0b.at[m, after(k)], tx.at[m, rows_of(me_u)],
            g_s.at[m, k - 1], g_r.at[m, k - 1], after(k), me_c,
        )

    def t_copy(m):
        return copy(
            tx.at[m], tc.at[:, pl.ds(pl.multiple_of(m * CB, CB), CB)],
            t_s.at[m], t_r.at[m], me_u, to_column(m),
        )

    def solve(first, last):
        @pl.loop(first, last)
        def _(n):
            m = tile(n)
            for v in range(U):
                block = dot(panel[0, m], dinv[0, v * CB : (v + 1) * CB, :], NT)
                t0f[m, :, v * CB : (v + 1) * CB] = block
                t0b[m, v] = block.astype(BF16)

            @pl.when(n < sends)
            def _():
                for k in range(1, U):
                    g_copy(m, k).start()
                tx[m, rows_of(me_u), :] = t0b[m, me_u]

    def forward(first, last):
        @pl.loop(first, last)
        def _(n):
            @pl.when(n < sends)
            def _():
                m = tile(n)
                for k in range(1, U):
                    region = tx.at[m, rows_of(before(k))]
                    copy(
                        region, region, g_s.at[m, k - 1], g_r.at[m, k - 1], after(k), me_c
                    ).wait_recv()
                t_copy(m).start()

    solve(0, min(2, M))

    @pl.loop(0, M)
    def _(t):
        probe = (dot(sketch[0], vf[0, t, 0], NT) * keep[t]).astype(BF16)
        r[t] = dot(probe, uf[0, t, 0], NN).astype(BF16)

    for k in range(1, U):
        scatter_out(r, k, r_rx, r_s, r_r).start()

    solve(min(2, M), M)
    forward(0, min(2, M))

    for k in range(1, U):
        scatter_out(r, k, r_rx, r_s, r_r).wait_recv()
    forward(min(2, M), min(4, M))

    summed = r[own].astype(F32)
    for k in range(1, U):
        summed = summed + r_rx[k - 1].astype(F32)
    zeros = jnp.zeros((K, B), F32)
    at_row = lax.broadcasted_iota(jnp.int32, (K, 2 * K), 0)
    at_col = lax.broadcasted_iota(jnp.int32, (K, 2 * K), 1)
    eye = jnp.where(at_col == at_row + K, 1.0, 0.0).astype(F32)
    grams = [
        dot_high(summed[i], jnp.concatenate([summed[i], zeros], axis=0), NT) + eye
        for i in range(MT)
    ]
    inverse = inverse_factor(jnp.stack(grams))
    for i in range(MT):
        basis[me_u * MT + i] = dot_high(
            inverse[i], jnp.concatenate([zeros, summed[i]], axis=0), NN
        ).astype(BF16)

    def gather_out(buf, k, send, recv):
        return copy(buf.at[own], buf.at[own], send.at[k - 1], recv.at[k - 1], after(k), me_c)

    def gather_in(buf, k, send, recv):
        region = buf.at[tiles(before(k))]
        return copy(region, region, send.at[k - 1], recv.at[k - 1], after(k), me_c)

    for k in range(1, U):
        gather_out(basis, k, b_s, b_r).start()

    def b_copy(i):
        m = me_u * MT + i
        return copy(basis.at[m], bf.at[i, 0], bx_s.at[i], bx_r.at[i], me_u, to_column(m))

    for i in range(MT):
        @pl.when(to_column(me_u * MT + i) < C)
        def _():
            b_copy(i).start()

    forward(min(4, M), M)
    for k in range(1, U):
        gather_in(basis, k, b_s, b_r).wait_recv()

    def project(t):
        coeff = (dot(basis[t], uf[0, t, 0], NT) * keep[t]).astype(BF16)
        xp[t] = dot(coeff, vf[0, t, 0], NN).astype(BF16)

    @pl.loop(0, M)
    def _(t):
        project(t)

    for k in range(1, U):
        scatter_out(xp, k, x_rx, x_s, x_r).start()

    for k in range(1, U):
        scatter_out(xp, k, x_rx, x_s, x_r).wait_recv()

    cross = xp[own].astype(F32)
    for k in range(1, U):
        cross = cross + x_rx[k - 1].astype(F32)
    cross = cross.astype(BF16)
    for i in range(MT):
        for v in range(U):
            e[me_u * MT + i, v] = dot(
                cross[i], dinv[0, v * CB : (v + 1) * CB, :], NT
            ).astype(BF16)

    for k in range(1, U):
        gather_out(e, k, e_s, e_r).start()
    for k in range(1, U):
        gather_in(e, k, e_s, e_r).wait_recv()

    def f_copy(m, i):
        return copy(
            f.at[m], bf.at[i, 1, :, pl.ds(pl.multiple_of(me_u * RD, RD), RD)],
            f_s.at[m], f_r.at[i, me_u], m // MT, to_column(m),
        )

    for m in range(M):
        @pl.when(to_column(m) < C)
        def _():
            rows = basis[m, :, pl.ds(pl.multiple_of(me_u * RD, RD), RD)]
            left = jnp.zeros((K, RD), F32)
            square = jnp.zeros((K, K), F32)
            for v in range(U):
                left = left + dot(e[m, v], t0b[m, v], NT)
                square = square + dot(e[m, v], e[m, v], NT)
            f[m] = (left - 0.5 * dot_high(square, rows.astype(F32), NN)).astype(BF16)
            f_copy(m, m % MT).start()

    @pl.loop(0, M)
    def _(m):
        rows = basis[m, :, pl.ds(pl.multiple_of(me_u * RD, RD), RD)]
        for v in range(U):
            cols = slice(v * CB, (v + 1) * CB)
            out[0, m, :, cols] = (t0f[m, :, cols] - dot(rows, e[m, v], TN)).astype(BF16)

    for m in range(M):
        cols = slice(m * CB, (m + 1) * CB)

        @pl.when(me_c - m - 1 >= 0)
        def _():
            t_copy(m).wait_recv()

        @pl.when(me_c - m - 1 < 0)
        def _():
            tc[:, cols] = jnp.zeros((B, CB), BF16)

    @pl.loop(0, U)
    def _(u):
        acc[rows_of(u), :] = dot(tc[rows_of(u), :], tc[...], NT)

    for i in range(MT):
        @pl.when(me_c - (me_u * MT + i) - 1 >= 0)
        def _():
            b_copy(i).wait_recv()

            @pl.loop(0, U)
            def _(s):
                copy(
                    f.at[0], bf.at[i, 1, :, pl.ds(pl.multiple_of(s * RD, RD), RD)],
                    f_s.at[0], f_r.at[i, s], me_u, me_c,
                ).wait_recv()

        @pl.when(me_c - (me_u * MT + i) - 1 < 0)
        def _():
            bf[i] = jnp.zeros((2, K, B), BF16)

    for i in range(MT):
        for n in range(2):
            pair[i, n] = bf[i, 1 - n]

    def product(u):
        left = bf[:, :, :, rows_of(u)].reshape(2 * MT * K, RD)
        return acc[rows_of(u), :] - dot(left, pair[...].reshape(2 * MT * K, B), TN)

    X = U // 2
    side = lax.rem(me_u, 2)
    partner = me_u + 1 - 2 * side

    def ahead(k):
        return lax.rem(me_u + 2 * k, U)

    def near_copy(k):
        return copy(near.at[k], near_rx.at[k], near_s.at[k], near_r.at[k], partner, me_c)

    def far_copy(k):
        return copy(
            far.at[k - 1], far_rx.at[k - 1], far_s.at[k - 1], far_r.at[k - 1], ahead(k), me_c
        )

    for n in range(1, X + 1):
        k = n % X
        near[k] = product(ahead(k) + 1 - 2 * side).astype(BF16)
        near_copy(k).start()
    for k in range(1, X):
        part = product(ahead(k))
        near_copy(k).wait_recv()
        far[k - 1] = (part + near_rx[k].astype(F32)).astype(BF16)
        far_copy(k).start()
    part = diag[0].astype(F32) - product(me_u)
    near_copy(0).wait_recv()
    diag_out[0] = part - near_rx[0].astype(F32)
    for k in range(1, X):
        far_copy(k).wait_recv()
        diag_out[0] = diag_out[0] - far_rx[k - 1].astype(F32)

    for k in range(1, U):
        scatter_out(r, k, r_rx, r_s, r_r).wait_send()
        gather_out(basis, k, b_s, b_r).wait_send()
        scatter_out(xp, k, x_rx, x_s, x_r).wait_send()
        gather_out(e, k, e_s, e_r).wait_send()
    for k in range(X):
        near_copy(k).wait_send()
    for k in range(1, X):
        far_copy(k).wait_send()
    for i in range(MT):
        @pl.when(to_column(me_u * MT + i) < C)
        def _():
            b_copy(i).wait_send()

    @pl.loop(0, M)
    def _(m):
        @pl.when(to_column(m) < C)
        def _():
            for k in range(1, U):
                g_copy(m, k).wait_send()
            t_copy(m).wait_send()
            f_copy(m, lax.rem(m, MT)).wait_send()


def local(U, C, panel, diag_tiles, dinv, u_fac, v_fac, ranks, sketch):
    M, RD, B = panel.shape[1:]
    R = u_fac.shape[3]
    K = sketch.shape[1]
    CB, MT, X = B // U, M // U, U // 2
    slots = lax.broadcasted_iota(jnp.int32, (M, 1, R), 2)
    keep = (slots < ranks[0, :, 0][:, None, None]).astype(F32)
    dma = pltpu.SemaphoreType.DMA
    peers = [dma((U - 1,))] * 2
    vmem = pl.BlockSpec(memory_space=pltpu.VMEM)
    return pl.pallas_call(
        functools.partial(kernel, U, C),
        out_shape=(
            jax.ShapeDtypeStruct(panel.shape, BF16),
            jax.ShapeDtypeStruct(diag_tiles.shape, F32),
        ),
        in_specs=[vmem] * 7,
        out_specs=(vmem, vmem),
        scratch_shapes=[
            pltpu.VMEM((M, RD, B), F32),
            pltpu.VMEM((M, U, RD, CB), BF16),
            pltpu.VMEM((M, B, CB), BF16),
            pltpu.VMEM((B, M * CB), BF16),
            pltpu.VMEM((MT, 2, K, B), BF16),
            pltpu.VMEM((MT, 2, K, B), BF16),
            pltpu.VMEM((M, K, RD), BF16),
            pltpu.VMEM((M, K, B), BF16),
            pltpu.VMEM((U - 1, MT, K, B), BF16),
            pltpu.VMEM((M, K, B), BF16),
            pltpu.VMEM((M, K, B), BF16),
            pltpu.VMEM((U - 1, MT, K, B), BF16),
            pltpu.VMEM((M, U, K, CB), BF16),
            pltpu.VMEM((B, B), F32),
            pltpu.VMEM((X, RD, B), BF16),
            pltpu.VMEM((X, RD, B), BF16),
            pltpu.VMEM((X - 1, RD, B), BF16),
            pltpu.VMEM((X - 1, RD, B), BF16),
            dma((M, U - 1)), dma((M, U - 1)), dma((M,)), dma((M,)), dma((MT,)), dma((MT,)), dma((M,)), dma((MT, U)),
            *peers, *peers, *peers, *peers,
            dma((X,)), dma((X,)), dma((X - 1,)), dma((X - 1,)),
        ],
        compiler_params=pltpu.CompilerParams(
            collective_id=0, has_side_effects=True, vmem_limit_bytes=58 * 1024 * 1024
        ),
        name="band_window",
    )(panel, diag_tiles, dinv, u_fac, v_fac, keep, sketch)


def solution(mesh):
    in_specs = (
        P("col", None, "upd", None),
        P("col", "upd", None),
        P("col", None, None),
        P("col", None, "upd", None, None),
        P("col", None, "upd", None, None),
        P("col", None, "upd"),
        P("col", None, None),
    )
    out_specs = (P("col", None, "upd", None), P("col", "upd", None))
    body = functools.partial(local, mesh.shape["upd"], mesh.shape["col"])
    return jax.shard_map(body, mesh=mesh, in_specs=in_specs, out_specs=out_specs, check_vma=False)
```
